512 devices in a mesh: seq: 64 (over y, z_hi, x), tp: 8 (over z_lo, core).
Axes of the slice: x: 4, y: 4, z: 16 (z_hi: 4, z_lo: 4; z = z_hi * 4 + z_lo), core: 2. Of those that a mesh axis runs over, the one named last changes fastest.
Arguments:
- tokens: bfloat16 [8192, 4096], P('seq'), may hold values from -6 to 6
- w_value: bfloat16 [4096, 4096], P('seq', 'tp'), may hold values from -0.09375 to 0.09375
- w_gate: bfloat16 [4096, 4096], P('seq', 'tp'), may hold values from -0.09375 to 0.09375
- w_output: bfloat16 [4096, 4096], P('tp', 'seq'), may hold values from -0.09375 to 0.09375
- residues: float32 [8, 64, 8, 16], P('tp', 'seq'), may hold values from -1.5 to 1.5
- log_rates: float32 [8, 64, 8, 16], P('tp', 'seq'), as said below
- cotangent: bfloat16 [8192, 4096], P('seq'), may hold values from -6 to 6
Outputs:
- layer_out: bfloat16 [8192, 4096], P('seq', 'tp')
- token_grad: bfloat16 [8192, 4096], P('seq', 'tp')
- residue_grad: float32 [8, 64, 8, 16], P('tp', 'seq')
- log_rate_grad: float32 [8, 64, 8, 16], P('tp', 'seq')
The draws below stay inside these ranges and needn't reach their ends.
Inputs may be any that keep to these rules, and one draw needn't show every extreme that they name: log_rates lie between log(0.5 / 8192) and log(1 / 24).
All inputs are finite; a program needn't handle non-finite values.
Results may differ from the reference program's by a relative error of at most 0.018.
Values may be sent and summed in bfloat16 or wider, within the bound.
No kernel may reach another device: no remote copies, remote signals or barrier semaphores. Data moves between devices by JAX's collectives and lax.ppermute only.
A program may use at most 64 MiB of HBM per device.

```python
import math
import jax
import jax.numpy as jnp
from jax import lax

D = 4096
R = 16
SEQ = 8192
CH = 8
N_SEQ = 64
N_TP = 8


def draw_log_rates(key, part):
    key = jax.random.fold_in(key, 7)
    shape = (N_TP, N_SEQ, CH, R)
    lowest = math.log(0.5 / SEQ)
    highest = math.log(1.0 / 24.0)
    return jax.random.uniform(key, shape, jnp.float32, lowest, highest).astype(jnp.float32)


def shard_levels(rng, dims, shards, low, top_value):
    gain, own = 1.0, jax.random.fold_in(rng, 6)
    for position, shards_of in shards:
        heights = jnp.exp(jax.random.uniform(jax.random.fold_in(own, position), (shards_of,), jnp.float32, low / len(shards), top_value / len(shards)))
        gain = gain * jnp.repeat(heights, dims[position] // shards_of).reshape([-1 if axis == position else 1 for axis in range(len(dims))])
    return gain


def gaussian(own_key, dims, width, bound, pieces=(), held_as=jnp.bfloat16):
    factor_of = shard_levels(own_key, dims, pieces, -0.22, 0.18) if pieces else 1.0
    drawn = jax.random.normal(own_key, dims, jnp.float32) * width * factor_of
    return jnp.minimum(jnp.maximum(drawn, -bound), bound).astype(held_as)


def setup_inputs(seed: int = 0) -> dict:
    key_list = jax.random.split(jax.random.key(seed), 8)
    return {
        "tokens": gaussian(key_list[0], (SEQ, D), 1.0, 6.0, ((0, 64),)),
        "w_value": gaussian(key_list[1], (D, D), D ** -0.5, 0.09375, ((0, 64), (1, 8))),
        "w_gate": gaussian(key_list[2], (D, D), D ** -0.5, 0.09375, ((0, 64), (1, 8))),
        "w_output": gaussian(key_list[3], (D, D), D ** -0.5, 0.09375, ((0, 8), (1, 64))),
        "residues": gaussian(key_list[4], (N_TP, N_SEQ, CH, R), R ** -0.5, 1.5, ((0, 8), (1, 64)), jnp.float32),
        "log_rates": draw_log_rates(jax.random.fold_in(key_list[7], 71), 0),
        "cotangent": gaussian(key_list[6], (SEQ, D), 1.0, 6.0, ((0, 64),)),
    }


def make_filter(residue_rows, log_rows, length):
    rates = jnp.exp(log_rows)
    offsets = jnp.arange(length).astype(jnp.float32)
    amplitude = residue_rows * jnp.sqrt(2.0 * rates)
    return lax.optimization_barrier(jnp.sum(amplitude[:, :, None] * jnp.exp(-rates[:, :, None] * offsets[None, None, :]), axis=1))

def exact_dot(left, right):
    return jnp.dot(left.astype(jnp.float32), right.astype(jnp.float32), precision=lax.Precision.HIGHEST, preferred_element_type=jnp.float32)

def reference(tokens, w_value, w_gate, w_output, residues, log_rates, cotangent):
    local_width = D // N_TP
    padded = 2 * SEQ
    scale = SEQ ** (-0.5)
    residue_blocks = residues.reshape(N_TP, local_width, R)
    rate_blocks = log_rates.reshape(N_TP, local_width, R)
    out_total = jnp.zeros((SEQ, D), jnp.float32)
    grad_total = jnp.zeros((SEQ, D), jnp.float32)
    residue_list = []
    rate_list = []
    for block in range(N_TP):
        value_weight = w_value[:, block * local_width:(block + 1) * local_width]
        gate_weight = w_gate[:, block * local_width:(block + 1) * local_width]
        output_weight = w_output[block * local_width:(block + 1) * local_width, :]
        residue_rows = residue_blocks[block]
        log_rows = rate_blocks[block]
        values = exact_dot(tokens, value_weight).astype(jnp.bfloat16)
        gates = exact_dot(tokens, gate_weight).T
        filters = make_filter(residue_rows, log_rows, SEQ)
        filter_spec = jnp.fft.rfft(filters, n=padded, axis=1)
        value_spec = jnp.fft.rfft(values.T.astype(jnp.float32), n=padded, axis=1)
        conv = jnp.fft.irfft(value_spec * filter_spec, n=padded, axis=1)[:, :SEQ].astype(jnp.bfloat16)
        mixed = (gates * conv.astype(jnp.float32)).astype(jnp.bfloat16)
        partial_out = exact_dot(mixed.T, output_weight).astype(jnp.bfloat16)
        partial_out = lax.optimization_barrier(partial_out).astype(jnp.float32)
        back = exact_dot(output_weight, cotangent.T)
        gate_grad = (back * conv.astype(jnp.float32)).astype(jnp.bfloat16)
        conv_grad = (back * gates).astype(jnp.bfloat16)
        grad_spec = jnp.fft.rfft(conv_grad.astype(jnp.float32), n=padded, axis=1)
        value_grad = jnp.fft.irfft(grad_spec * jnp.conj(filter_spec), n=padded, axis=1)[:, :SEQ].astype(jnp.bfloat16)
        filter_grad = jnp.fft.irfft(grad_spec * jnp.conj(value_spec), n=padded, axis=1)[:, :SEQ]

        def filter_of(first_arg, second_arg):
            return make_filter(first_arg, second_arg, SEQ)
        unused, pullback = jax.vjp(filter_of, residue_rows, log_rows)
        residue_grad, rate_grad = pullback(filter_grad.astype(unused.dtype))
        partial_grad = exact_dot(value_grad.T, value_weight.T) + exact_dot(gate_grad.T, gate_weight.T)
        partial_grad = lax.optimization_barrier(partial_grad.astype(jnp.bfloat16)).astype(jnp.float32)
        out_total = out_total + partial_out
        grad_total = grad_total + partial_grad
        residue_list.append(residue_grad * scale)
        rate_list.append(rate_grad * scale)
    residue_grads = jnp.stack(residue_list, axis=0)
    rate_grads = jnp.stack(rate_list, axis=0)
    return (out_total.astype(jnp.bfloat16), grad_total.astype(jnp.bfloat16), residue_grads.reshape(N_TP, N_SEQ, CH, R), rate_grads.reshape(N_TP, N_SEQ, CH, R))
```

```python
import jax
import jax.numpy as jnp
from jax import lax
from jax.experimental import pallas as pl
from jax.experimental.pallas import tpu as pltpu
from jax.sharding import PartitionSpec as P

EXACT = lax.Precision.HIGHEST
VMEM_GRANT = 56 * 2**20


def groups_along(sizes, picked):
    groups = {}
    total = 1
    for size in sizes:
        total *= size
    for index in range(total):
        rest, coords = index, []
        for size in reversed(sizes):
            coords.append(rest % size)
            rest //= size
        coords.reverse()
        key = tuple(c for axis, c in enumerate(coords) if axis not in picked)
        groups.setdefault(key, []).append(index)
    return list(groups.values())


def exchange(blocks, axis, groups=None):
    return lax.all_to_all(
        blocks, axis, split_axis=0, concat_axis=0, tiled=True, axis_index_groups=groups
    )


def batched(spec, left, right):
    return jnp.einsum(spec, left, right, precision=EXACT, preferred_element_type=jnp.float32)


def mode_tables(residue_rows, log_rows, chunks, width):
    rates = jnp.exp(log_rows)
    root = jnp.sqrt(2.0 * rates)
    amplitude = residue_rows * root
    channels, modes = rates.shape
    steps = jnp.arange(width).astype(jnp.float32)
    lag = steps[None, :] - steps[:, None]
    to_end = width - 1.0 - steps
    grow = jnp.exp(rates[:, :, None] * steps[None, None, :])
    fade = jnp.exp(-rates[:, :, None] * steps[None, None, :])
    near = batched("cru,crt->cut", amplitude[:, :, None] * grow, fade)
    near = jnp.where((lag >= 0.0)[None], near, 0.0)
    into = jnp.exp(-rates[:, :, None] * to_end[None, None, :])
    out_of = jnp.exp(-rates[:, :, None] * (steps + 1.0)[None, None, :])

    def wide(table):
        own = jnp.eye(channels, dtype=jnp.float32)[:, :, None, None]
        return (own * table[None]).reshape(channels, channels * modes, width)

    filters = jnp.stack(
        [
            wide(into).swapaxes(1, 2),
            wide(out_of).swapaxes(1, 2),
            near,
            near.swapaxes(1, 2),
            wide(amplitude[:, :, None] * out_of),
            wide(amplitude[:, :, None] * into),
        ]
    )
    high = lax.reduce_precision(filters, 8, 7)
    low = (filters - high).astype(jnp.bfloat16)
    spans = width * 2.0 ** jnp.arange(8).astype(jnp.float32)
    hops = jnp.exp(-rates.reshape(1, -1) * spans[:, None])
    return {
        "rates": rates,
        "root": root,
        "grow": grow,
        "fade": fade,
        "into": into,
        "out_of": out_of,
        "high": high.astype(jnp.bfloat16),
        "low": low,
        "hops": hops,
    }


def filter_kernel(signal, high, low, hops, filtered, states):
    channels, chunks = signal.shape[1:3]
    modes = hops.shape[1]

    def dot(left, right):
        return jnp.dot(left, right, preferred_element_type=jnp.float32)

    def times(left, table, c):
        return dot(left, high[table, c]) + dot(left, low[table, c])

    head = jnp.zeros((chunks, modes), jnp.float32)
    tail = jnp.zeros((chunks, modes), jnp.float32)
    for c in range(channels):
        head = head + times(signal[0, c], 0, c)
        tail = tail + times(signal[1, c], 1, c)
    place = lax.broadcasted_iota(jnp.int32, (chunks, modes), 0)

    def later(array, step):
        return jnp.where(place >= step, pltpu.roll(array, step, 0), 0.0)

    def earlier(array, step):
        return jnp.where(place < chunks - step, pltpu.roll(array, chunks - step, 0), 0.0)

    ahead, behind = later(head, 1), earlier(tail, 1)
    step, level = 1, 0
    while step < chunks:
        hop = hops[level : level + 1, :]
        ahead = ahead + hop * later(ahead, step)
        behind = behind + hop * earlier(behind, step)
        step, level = 2 * step, level + 1
    states[0], states[1], states[2] = head, tail, ahead
    for which, state in ((0, ahead), (1, behind)):
        rough = state.astype(jnp.bfloat16)
        fine = (state - rough.astype(jnp.float32)).astype(jnp.bfloat16)
        for c in range(channels):
            far = times(rough, 4 + which, c) + dot(fine, high[4 + which, c])
            filtered[which, c] = (times(signal[which, c], 2 + which, c) + far).astype(jnp.bfloat16)


def filter_both(signal, tables):
    channels, chunks = signal.shape[1:3]
    modes = tables["hops"].shape[1]
    return pl.pallas_call(
        filter_kernel,
        out_shape=(
            jax.ShapeDtypeStruct(signal.shape, jnp.bfloat16),
            jax.ShapeDtypeStruct((3, chunks, modes), jnp.float32),
        ),
        in_specs=[pl.BlockSpec(memory_space=pltpu.VMEM)] * 4,
        out_specs=(pl.BlockSpec(memory_space=pltpu.VMEM),) * 2,
        compiler_params=pltpu.CompilerParams(vmem_limit_bytes=24 * 2**20),
        cost_estimate=pl.CostEstimate(flops=200_000_000, bytes_accessed=4_000_000, transcendentals=0),
    )(signal, tables["high"], tables["low"], tables["hops"])


def fetch(weights, held, arrived):
    side_y, _, side_z = weights.shape[:3]
    copies = [
        pltpu.make_async_copy(
            weights.at[i // side_z, :, i % side_z], held.at[i], arrived.at[i]
        )
        for i in range(side_y * side_z)
    ]
    for copy in copies:
        copy.start()

    def block(i):
        copies[i].wait()
        return held[i].reshape(-1, held.shape[3])

    return block


def project_kernel(
    tokens, cotangent, weights, gates, back, sent, held, arrived, total, back_total
):
    width = gates.shape[0]
    block = fetch(weights, held, arrived)
    depth = held.shape[1] * held.shape[2]
    for i in range(held.shape[0]):
        rows = block(i)
        columns = slice(i * depth, (i + 1) * depth)
        term = jnp.dot(
            tokens[:, columns], rows[:, : 2 * width], preferred_element_type=jnp.float32
        )
        back_term = jnp.dot(
            cotangent[:, columns], rows[:, 2 * width :], preferred_element_type=jnp.float32
        )
        if i == 0:
            total[...] = term
            back_total[...] = back_term
        else:
            total[...] += term
            back_total[...] += back_term
    gates[...] = total[:, width:].T
    back[...] = back_total[...].T
    sent[0] = total[:, :width].T.astype(jnp.bfloat16)
    sent[1] = (back[...] * gates[...]).astype(jnp.bfloat16)


def held_blocks(weights):
    side_y, side_x, side_z, deep, wide = weights.shape
    return [
        pltpu.VMEM((side_y * side_z, side_x, deep, wide), weights.dtype),
        pltpu.SemaphoreType.DMA((side_y * side_z,)),
    ]


def project(tokens, cotangent, weights):
    rows = tokens.shape[0]
    width = weights.shape[4] // 3
    here = pl.BlockSpec(memory_space=pltpu.VMEM)
    return pl.pallas_call(
        project_kernel,
        out_shape=(
            jax.ShapeDtypeStruct((width, rows), jnp.float32),
            jax.ShapeDtypeStruct((width, rows), jnp.float32),
            jax.ShapeDtypeStruct((2, width, rows), jnp.bfloat16),
        ),
        in_specs=[here, here, pl.BlockSpec(memory_space=pl.ANY)],
        out_specs=(here, here, here),
        scratch_shapes=held_blocks(weights)
        + [
            pltpu.VMEM((rows, 2 * width), jnp.float32),
            pltpu.VMEM((rows, width), jnp.float32),
        ],
        compiler_params=pltpu.CompilerParams(vmem_limit_bytes=VMEM_GRANT),
    )(tokens, cotangent, weights)


def out_kernel(gates, back, filtered, weights, parts, held, arrived, mixed, grads):
    width = gates.shape[0]
    block = fetch(weights, held, arrived)
    conv = filtered[0].astype(jnp.float32)
    mixed[...] = (gates[...] * conv).astype(jnp.bfloat16)
    grads[:width] = filtered[1]
    grads[width:] = (back[...] * conv).astype(jnp.bfloat16)
    side_y, side_z = weights.shape[0], weights.shape[2]
    depth = held.shape[1] * held.shape[2]
    for i in range(side_y * side_z):
        y, z = i // side_z, i % side_z
        rows = block(i)
        columns = slice(z % 2 * depth, (z % 2 + 1) * depth)
        out = jnp.dot(rows[:, 2 * width :], mixed[...], preferred_element_type=jnp.float32)
        parts[z // 2, y, 0, :, columns] = out.T.astype(jnp.bfloat16)
        out = jnp.dot(rows[:, : 2 * width], grads[...], preferred_element_type=jnp.float32)
        parts[z // 2, y, 1, :, columns] = out.T.astype(jnp.bfloat16)


def project_back(gates, back, filtered, weights):
    width, rows = gates.shape
    side_y, side_x, side_z, deep, _ = weights.shape
    here = pl.BlockSpec(memory_space=pltpu.VMEM)
    return pl.pallas_call(
        out_kernel,
        out_shape=jax.ShapeDtypeStruct(
            (side_z // 2, side_y, 2, rows, 2 * side_x * deep), jnp.bfloat16
        ),
        in_specs=[here, here, here, pl.BlockSpec(memory_space=pl.ANY)],
        out_specs=here,
        scratch_shapes=held_blocks(weights)
        + [
            pltpu.VMEM((width, rows), jnp.bfloat16),
            pltpu.VMEM((2 * width, rows), jnp.bfloat16),
        ],
        compiler_params=pltpu.CompilerParams(vmem_limit_bytes=VMEM_GRANT),
    )(gates, back, filtered, weights)


def by_chunk(states):
    return states.reshape(-1, states.shape[2]).T


def parameter_grads(signal, grad, head, tail, ahead, residue_rows, tables):
    chunks, width = signal.shape[1:]
    steps = jnp.arange(width).astype(jnp.float32)
    lag = jnp.maximum(steps[None, :] - steps[:, None], -1.0)[None]
    overlap = jnp.where(lag >= 0.0, batched("cku,ckt->cut", signal, grad), 0.0)
    grow, fade = tables["grow"], tables["fade"]
    shape = residue_rows.shape
    plain = jnp.sum(batched("cut,crt->cru", overlap, fade) * grow, axis=2)
    plain = plain + jnp.sum(ahead * tail, axis=0).reshape(shape)
    into_moment = tables["into"] * (width - 1.0 - steps)[None, None, :]
    out_moment = tables["out_of"] * (steps + 1.0)[None, None, :]
    head_moment = by_chunk(batched("cku,cru->crk", signal, into_moment))
    tail_moment = by_chunk(batched("ckt,crt->crk", grad, out_moment))
    blocks = jnp.arange(chunks).astype(jnp.float32)
    gap = (blocks[:, None] - blocks[None, :] - 1.0)[:, :, None]
    hop = width * jnp.maximum(gap, 0.0)
    carry = jnp.where(gap >= 0.0, jnp.exp(-tables["rates"].reshape(1, 1, -1) * hop), 0.0)
    ahead_moment = jnp.sum(carry * (head_moment[None] + hop * head[None]), axis=1)
    far = jnp.sum(ahead * tail_moment + ahead_moment * tail, axis=0).reshape(shape)
    moment = jnp.sum(batched("cut,crt->cru", overlap * lag, fade) * grow, axis=2) + far
    root = tables["root"]
    return plain * root, residue_rows * root * (0.5 * plain - tables["rates"] * moment)


def local(tokens, w_value, w_gate, w_output, residues, log_rates, cotangent):
    seq_devices, tp_devices = lax.axis_size("seq"), lax.axis_size("tp")
    side = 4
    sizes, tp_sizes = (side, side, seq_devices // side**2), (tp_devices // 2, 2)
    z_groups, yx_groups = groups_along(sizes, (1,)), groups_along(sizes, (0, 2))
    core_groups, line_groups = groups_along(tp_sizes, (1,)), groups_along(tp_sizes, (0,))
    rows, model = tokens.shape
    block, width = w_value.shape
    channels = width // seq_devices
    half = jnp.bfloat16

    weights = jnp.concatenate([w_value, w_gate, w_output.T], axis=1)
    along_z = lax.all_gather(weights, "seq", axis=0, tiled=True, axis_index_groups=z_groups)

    along_z, residues, log_rates = lax.optimization_barrier((along_z, residues, log_rates))
    full = lax.all_gather(along_z, "seq", axis=0, tiled=True, axis_index_groups=yx_groups)
    residue_rows = residues.reshape(channels, residues.shape[3])
    log_rows = log_rates.reshape(channels, log_rates.shape[3])
    tables = mode_tables(residue_rows, log_rows, seq_devices, rows)
    full, tables = lax.optimization_barrier((full, tables))
    full = full.reshape(side, side, side, block, 3 * width)

    gates, back, sent = project(tokens, cotangent, full)
    sent = sent.reshape(2, seq_devices, channels, rows).swapaxes(0, 1)
    got = exchange(sent, "seq").transpose(1, 2, 0, 3)
    filtered, states = filter_both(got, tables)
    got_back = exchange(filtered.transpose(2, 0, 1, 3), "seq")
    got_back = got_back.swapaxes(0, 1).reshape(2, width, rows)
    parts = project_back(gates, back, got_back, full)

    pair = exchange(parts, "tp", core_groups).astype(jnp.float32)
    pair = (pair[0] + pair[1]).astype(half)
    pair, got, states = lax.optimization_barrier((pair, got, states))
    line = exchange(pair, "tp", line_groups).astype(jnp.float32)
    summed = ((line[0] + line[1]) + (line[2] + line[3])).astype(half)
    result = summed.reshape(2, rows, model // tp_devices)

    signal, grad = got[0].astype(jnp.float32), got[1].astype(jnp.float32)
    residue_grad, rate_grad = parameter_grads(
        signal, grad, states[0], states[1], states[2], residue_rows, tables
    )
    scale = (rows * seq_devices) ** (-0.5)
    return (
        result[0],
        result[1],
        (residue_grad * scale).reshape(residues.shape),
        (rate_grad * scale).reshape(log_rates.shape),
    )


def solution(mesh):
    in_specs = (
        P("seq", None),
        P("seq", "tp"),
        P("seq", "tp"),
        P("tp", "seq"),
        P("tp", "seq", None, None),
        P("tp", "seq", None, None),
        P("seq", None),
    )
    out_specs = (
        P("seq", "tp"),
        P("seq", "tp"),
        P("tp", "seq", None, None),
        P("tp", "seq", None, None),
    )
    return jax.shard_map(local, mesh=mesh, in_specs=in_specs, out_specs=out_specs, check_vma=False)
```

```python
import jax
import jax.numpy as jnp
from jax import lax
from jax.experimental import pallas as pl
from jax.experimental.pallas import tpu as pltpu
from jax.sharding import PartitionSpec as P

EXACT = lax.Precision.HIGHEST
VMEM_GRANT = 56 * 2**20


def groups_along(sizes, picked):
    groups = {}
    total = 1
    for size in sizes:
        total *= size
    for index in range(total):
        rest, coords = index, []
        for size in reversed(sizes):
            coords.append(rest % size)
            rest //= size
        coords.reverse()
        key = tuple(c for axis, c in enumerate(coords) if axis not in picked)
        groups.setdefault(key, []).append(index)
    return list(groups.values())


def exchange(blocks, axis, groups=None):
    return lax.all_to_all(
        blocks, axis, split_axis=0, concat_axis=0, tiled=True, axis_index_groups=groups
    )


def shift_pairs(sizes, axis, step):
    pairs = []
    for group in groups_along(sizes, (axis,)):
        pairs += [(group[i], group[(i + step) % len(group)]) for i in range(len(group))]
    return pairs


def shifted(array, sizes, axis, step):
    return lax.ppermute(array, "seq", shift_pairs(sizes, axis, step))


def gather_blocks(own, sizes, near_axis, far_axis):
    up = shifted(own, sizes, near_axis, -1)
    down = shifted(own, sizes, near_axis, 1)
    across = shifted(own, sizes, near_axis, 2)
    first, second = jnp.concatenate([own, up]), jnp.concatenate([across, down])
    first_down = shifted(first, sizes, far_axis, 1)
    second_up = shifted(second, sizes, far_axis, -1)
    second_down = shifted(second, sizes, far_axis, 1)
    first_up = shifted(first, sizes, far_axis, -1)
    first_across = shifted(first_down, sizes, far_axis, 1)
    second_across = shifted(second_up, sizes, far_axis, -1)
    return [
        first, second, first_up, second_up, first_across, second_across, first_down, second_down
    ]


def batched(spec, left, right):
    return jnp.einsum(spec, left, right, precision=EXACT, preferred_element_type=jnp.float32)


def mode_tables(residue_rows, log_rows, chunks, width):
    rates = jnp.exp(log_rows)
    root = jnp.sqrt(2.0 * rates)
    amplitude = residue_rows * root
    channels, modes = rates.shape
    steps = jnp.arange(width).astype(jnp.float32)
    lag = steps[None, :] - steps[:, None]
    to_end = width - 1.0 - steps
    grow = jnp.exp(rates[:, :, None] * steps[None, None, :])
    fade = jnp.exp(-rates[:, :, None] * steps[None, None, :])
    near = batched("cru,crt->cut", amplitude[:, :, None] * grow, fade)
    near = jnp.where((lag >= 0.0)[None], near, 0.0)
    into = jnp.exp(-rates[:, :, None] * to_end[None, None, :])
    out_of = jnp.exp(-rates[:, :, None] * (steps + 1.0)[None, None, :])

    def wide(table):
        own = jnp.eye(channels, dtype=jnp.float32)[:, :, None, None]
        return (own * table[None]).reshape(channels, channels * modes, width)

    filters = jnp.stack(
        [
            wide(into).swapaxes(1, 2),
            wide(out_of).swapaxes(1, 2),
            near,
            near.swapaxes(1, 2),
            wide(amplitude[:, :, None] * out_of),
            wide(amplitude[:, :, None] * into),
        ]
    )
    high = lax.reduce_precision(filters, 8, 7)
    low = (filters - high).astype(jnp.bfloat16)
    spans = width * 2.0 ** jnp.arange(8).astype(jnp.float32)
    hops = jnp.exp(-rates.reshape(1, -1) * spans[:, None])
    return {
        "rates": rates,
        "root": root,
        "grow": grow,
        "fade": fade,
        "into": into,
        "out_of": out_of,
        "high": high.astype(jnp.bfloat16),
        "low": low,
        "hops": hops,
    }


def filter_kernel(signal, high, low, hops, filtered, states):
    channels, chunks = signal.shape[1:3]
    modes = hops.shape[1]

    def dot(left, right):
        return jnp.dot(left, right, preferred_element_type=jnp.float32)

    def times(left, table, c):
        return dot(left, high[table, c]) + dot(left, low[table, c])

    head = jnp.zeros((chunks, modes), jnp.float32)
    tail = jnp.zeros((chunks, modes), jnp.float32)
    for c in range(channels):
        head = head + times(signal[0, c], 0, c)
        tail = tail + times(signal[1, c], 1, c)
    place = lax.broadcasted_iota(jnp.int32, (chunks, modes), 0)

    def later(array, step):
        return jnp.where(place >= step, pltpu.roll(array, step, 0), 0.0)

    def earlier(array, step):
        return jnp.where(place < chunks - step, pltpu.roll(array, chunks - step, 0), 0.0)

    ahead, behind = later(head, 1), earlier(tail, 1)
    step, level = 1, 0
    while step < chunks:
        hop = hops[level : level + 1, :]
        ahead = ahead + hop * later(ahead, step)
        behind = behind + hop * earlier(behind, step)
        step, level = 2 * step, level + 1
    states[0], states[1], states[2] = head, tail, ahead
    for which, state in ((0, ahead), (1, behind)):
        rough = state.astype(jnp.bfloat16)
        fine = (state - rough.astype(jnp.float32)).astype(jnp.bfloat16)
        for c in range(channels):
            far = times(rough, 4 + which, c) + dot(fine, high[4 + which, c])
            filtered[which, c] = (times(signal[which, c], 2 + which, c) + far).astype(jnp.bfloat16)


def filter_both(signal, tables):
    channels, chunks = signal.shape[1:3]
    modes = tables["hops"].shape[1]
    return pl.pallas_call(
        filter_kernel,
        out_shape=(
            jax.ShapeDtypeStruct(signal.shape, jnp.bfloat16),
            jax.ShapeDtypeStruct((3, chunks, modes), jnp.float32),
        ),
        in_specs=[pl.BlockSpec(memory_space=pltpu.VMEM)] * 4,
        out_specs=(pl.BlockSpec(memory_space=pltpu.VMEM),) * 2,
        compiler_params=pltpu.CompilerParams(vmem_limit_bytes=24 * 2**20),
        cost_estimate=pl.CostEstimate(flops=200_000_000, bytes_accessed=4_000_000, transcendentals=0),
    )(signal, tables["high"], tables["low"], tables["hops"])


SIDE = 4
COUNT = 4 * SIDE


def fetch(blocks, held, arrived):
    copies = [
        pltpu.make_async_copy(blocks[i], held.at[i], arrived.at[i]) for i in range(COUNT)
    ]
    for copy in copies:
        copy.start()

    def block(i):
        copies[i].wait()
        return held[i]

    return block


def split_index(i):
    return i // (2 * SIDE), i // 2 % SIDE, i % 2


def project_kernel(place, tokens, cotangent, turn, *refs):
    blocks, (gates, back, sent, held, arrived, total, back_total, turned) = refs[:COUNT], refs[COUNT:]
    width = gates.shape[0]
    block = fetch(blocks, held, arrived)
    deep = turn.shape[0]
    piece = deep // SIDE
    sources = (tokens, cotangent)
    for z1 in range(2):
        for distance in range(SIDE):
            y = lax.rem(place[0] + distance, SIDE)
            start = pl.multiple_of(y * (2 * deep) + z1 * deep, deep)
            for which in range(2):
                turned[which, z1, distance] = jnp.dot(
                    sources[which][:, pl.ds(start, deep)],
                    turn[...],
                    preferred_element_type=jnp.float32,
                ).astype(jnp.bfloat16)

    def columns(which, i):
        z1, far, half = split_index(i)
        if z1 == 0:
            return turned[which, 0, far, :, half * 2 * piece : (half + 1) * 2 * piece]
        lanes = slice(far * piece, (far + 1) * piece)
        return jnp.concatenate(
            [turned[which, 1, 2 * half, :, lanes], turned[which, 1, 2 * half + 1, :, lanes]], axis=1
        )

    for i in range(COUNT):
        rows = block(i)
        term = jnp.dot(columns(0, i), rows[:, : 2 * width], preferred_element_type=jnp.float32)
        back_term = jnp.dot(columns(1, i), rows[:, 2 * width :], preferred_element_type=jnp.float32)
        if i == 0:
            total[...] = term
            back_total[...] = back_term
        else:
            total[...] += term
            back_total[...] += back_term
    gates[...] = total[:, width:].T
    back[...] = back_total[...].T
    sent[0] = total[:, :width].T.astype(jnp.bfloat16)
    sent[1] = (back[...] * gates[...]).astype(jnp.bfloat16)


def held_blocks(blocks):
    return [
        pltpu.VMEM((COUNT,) + blocks[0].shape, blocks[0].dtype),
        pltpu.SemaphoreType.DMA((COUNT,)),
    ]


def project(place, tokens, cotangent, turn, blocks):
    rows = tokens.shape[0]
    width = blocks[0].shape[1] // 3
    here = pl.BlockSpec(memory_space=pltpu.VMEM)
    return pl.pallas_call(
        project_kernel,
        out_shape=(
            jax.ShapeDtypeStruct((width, rows), jnp.float32),
            jax.ShapeDtypeStruct((width, rows), jnp.float32),
            jax.ShapeDtypeStruct((2, width, rows), jnp.bfloat16),
        ),
        in_specs=[pl.BlockSpec(memory_space=pltpu.SMEM), here, here, here]
        + [pl.BlockSpec(memory_space=pl.ANY)] * COUNT,
        out_specs=(here, here, here),
        scratch_shapes=held_blocks(blocks)
        + [
            pltpu.VMEM((rows, 2 * width), jnp.float32),
            pltpu.VMEM((rows, width), jnp.float32),
            pltpu.VMEM((2, 2, SIDE, rows, turn.shape[0]), jnp.bfloat16),
        ],
        compiler_params=pltpu.CompilerParams(vmem_limit_bytes=VMEM_GRANT),
    )(place, tokens, cotangent, turn, *blocks)


def out_kernel(place, gates, back, filtered, *refs):
    blocks, (parts, held, arrived, mixed, grads) = refs[:COUNT], refs[COUNT:]
    width = gates.shape[0]
    block = fetch(blocks, held, arrived)
    conv = filtered[0].astype(jnp.float32)
    mixed[...] = (gates[...] * conv).astype(jnp.bfloat16)
    grads[:width] = filtered[1]
    grads[width:] = (back[...] * conv).astype(jnp.bfloat16)
    deep = held.shape[1]
    for i in range(COUNT):
        z1, far, half = split_index(i)
        rows = block(i)
        outs = (
            jnp.dot(rows[:, 2 * width :], mixed[...], preferred_element_type=jnp.float32),
            jnp.dot(rows[:, : 2 * width], grads[...], preferred_element_type=jnp.float32),
        )
        for which in range(2):
            out = outs[which].T.astype(jnp.bfloat16)
            if z1 == 0:
                y = lax.rem(place[0] + far, SIDE)
                parts[0, y, which, :, half * deep : (half + 1) * deep] = out
            else:
                for part in range(2):
                    y = lax.rem(place[0] + 2 * half + part, SIDE)
                    piece = slice(far * (deep // 2), (far + 1) * (deep // 2))
                    parts[1, y, which, :, piece] = out[:, part * (deep // 2) : (part + 1) * (deep // 2)]


def project_back(place, gates, back, filtered, blocks):
    width, rows = gates.shape
    deep = blocks[0].shape[0]
    here = pl.BlockSpec(memory_space=pltpu.VMEM)
    return pl.pallas_call(
        out_kernel,
        out_shape=jax.ShapeDtypeStruct((2, SIDE, 2, rows, 2 * deep), jnp.bfloat16),
        in_specs=[pl.BlockSpec(memory_space=pltpu.SMEM), here, here, here]
        + [pl.BlockSpec(memory_space=pl.ANY)] * COUNT,
        out_specs=here,
        scratch_shapes=held_blocks(blocks)
        + [
            pltpu.VMEM((width, rows), jnp.bfloat16),
            pltpu.VMEM((2 * width, rows), jnp.bfloat16),
        ],
        compiler_params=pltpu.CompilerParams(vmem_limit_bytes=VMEM_GRANT),
    )(place, gates, back, filtered, *blocks)


def by_chunk(states):
    return states.reshape(-1, states.shape[2]).T


def parameter_grads(signal, grad, head, tail, ahead, residue_rows, tables):
    chunks, width = signal.shape[1:]
    steps = jnp.arange(width).astype(jnp.float32)
    lag = jnp.maximum(steps[None, :] - steps[:, None], -1.0)[None]
    overlap = jnp.where(lag >= 0.0, batched("cku,ckt->cut", signal, grad), 0.0)
    grow, fade = tables["grow"], tables["fade"]
    shape = residue_rows.shape
    plain = jnp.sum(batched("cut,crt->cru", overlap, fade) * grow, axis=2)
    plain = plain + jnp.sum(ahead * tail, axis=0).reshape(shape)
    into_moment = tables["into"] * (width - 1.0 - steps)[None, None, :]
    out_moment = tables["out_of"] * (steps + 1.0)[None, None, :]
    head_moment = by_chunk(batched("cku,cru->crk", signal, into_moment))
    tail_moment = by_chunk(batched("ckt,crt->crk", grad, out_moment))
    blocks = jnp.arange(chunks).astype(jnp.float32)
    gap = (blocks[:, None] - blocks[None, :] - 1.0)[:, :, None]
    hop = width * jnp.maximum(gap, 0.0)
    carry = jnp.where(gap >= 0.0, jnp.exp(-tables["rates"].reshape(1, 1, -1) * hop), 0.0)
    ahead_moment = jnp.sum(carry * (head_moment[None] + hop * head[None]), axis=1)
    far = jnp.sum(ahead * tail_moment + ahead_moment * tail, axis=0).reshape(shape)
    moment = jnp.sum(batched("cut,crt->cru", overlap * lag, fade) * grow, axis=2) + far
    root = tables["root"]
    return plain * root, residue_rows * root * (0.5 * plain - tables["rates"] * moment)


def local(tokens, w_value, w_gate, w_output, residues, log_rates, cotangent):
    seq_devices, tp_devices = lax.axis_size("seq"), lax.axis_size("tp")
    sizes, tp_sizes = (SIDE, SIDE, seq_devices // SIDE**2), (tp_devices // 2, 2)
    z_groups = groups_along(sizes, (1,))
    core_groups, line_groups = groups_along(tp_sizes, (1,)), groups_along(tp_sizes, (0,))
    rows, model = tokens.shape
    block, width = w_value.shape
    channels = width // seq_devices
    half = jnp.bfloat16
    me = lax.axis_index("seq")

    weights = jnp.concatenate([w_value, w_gate, w_output.T], axis=1)
    along_z = lax.all_gather(weights, "seq", axis=0, tiled=True, axis_index_groups=z_groups)
    along_z = along_z.reshape(2, 2 * block, 3 * width)
    blocks = gather_blocks(along_z[0], sizes, 2, 0) + gather_blocks(along_z[1], sizes, 0, 2)

    place = (me // SIDE**2).reshape(1)
    deep = 2 * SIDE * block
    source, target = jnp.arange(deep)[:, None], jnp.arange(deep)[None, :]
    x_wanted = (me + target // (2 * block)) % SIDE
    wanted = target // block % 2 * (SIDE * block) + x_wanted * block + target % block
    turn = (source == wanted).astype(half)
    passed_on = [blocks[i] for i in (3, 6, 11, 14)]
    passed_on, residues, log_rates = lax.optimization_barrier((passed_on, residues, log_rates))
    residue_rows = residues.reshape(channels, residues.shape[3])
    log_rows = log_rates.reshape(channels, log_rates.shape[3])
    tables = mode_tables(residue_rows, log_rows, seq_devices, rows)
    blocks, tables, turn = lax.optimization_barrier((blocks, tables, turn))

    gates, back, sent = project(place, tokens, cotangent, turn, blocks)
    sent = sent.reshape(2, seq_devices, channels, rows).swapaxes(0, 1)
    got = exchange(sent, "seq").transpose(1, 2, 0, 3)
    filtered, states = filter_both(got, tables)
    got_back = exchange(filtered.transpose(2, 0, 1, 3), "seq")
    got_back = got_back.swapaxes(0, 1).reshape(2, width, rows)
    parts = project_back(place, gates, back, got_back, blocks)

    pair = exchange(parts, "tp", core_groups).astype(jnp.float32)
    pair = (pair[0] + pair[1]).astype(half)
    pair, got, states = lax.optimization_barrier((pair, got, states))
    line = exchange(pair, "tp", line_groups).astype(jnp.float32)
    summed = ((line[0] + line[1]) + (line[2] + line[3])).astype(half)
    result = lax.dot_general(
        summed.reshape(2 * rows, -1), turn, (((1,), (1,)), ((), ())), preferred_element_type=jnp.float32
    )
    result = result.astype(half).reshape(2, rows, model // tp_devices)

    signal, grad = got[0].astype(jnp.float32), got[1].astype(jnp.float32)
    residue_grad, rate_grad = parameter_grads(
        signal, grad, states[0], states[1], states[2], residue_rows, tables
    )
    scale = (rows * seq_devices) ** (-0.5)
    return (
        result[0],
        result[1],
        (residue_grad * scale).reshape(residues.shape),
        (rate_grad * scale).reshape(log_rates.shape),
    )


def solution(mesh):
    in_specs = (
        P("seq", None),
        P("seq", "tp"),
        P("seq", "tp"),
        P("tp", "seq"),
        P("tp", "seq", None, None),
        P("tp", "seq", None, None),
        P("seq", None),
    )
    out_specs = (
        P("seq", "tp"),
        P("seq", "tp"),
        P("tp", "seq", None, None),
        P("tp", "seq", None, None),
    )
    return jax.shard_map(local, mesh=mesh, in_specs=in_specs, out_specs=out_specs, check_vma=False)
```

```python
import jax
import jax.numpy as jnp
from jax import lax
from jax.experimental import pallas as pl
from jax.experimental.pallas import tpu as pltpu
from jax.sharding import PartitionSpec as P

EXACT = lax.Precision.HIGHEST
VMEM_GRANT = 56 * 2**20


def groups_along(sizes, picked):
    groups = {}
    total = 1
    for size in sizes:
        total *= size
    for index in range(total):
        rest, coords = index, []
        for size in reversed(sizes):
            coords.append(rest % size)
            rest //= size
        coords.reverse()
        key = tuple(c for axis, c in enumerate(coords) if axis not in picked)
        groups.setdefault(key, []).append(index)
    return list(groups.values())


def exchange(blocks, axis, groups=None):
    return lax.all_to_all(
        blocks, axis, split_axis=0, concat_axis=0, tiled=True, axis_index_groups=groups
    )


def shift_pairs(sizes, axis, step):
    pairs = []
    for group in groups_along(sizes, (axis,)):
        pairs += [(group[i], group[(i + step) % len(group)]) for i in range(len(group))]
    return pairs


def shifted(array, sizes, axis, step):
    return lax.ppermute(array, "seq", shift_pairs(sizes, axis, step))


def near_blocks(own, sizes, axis):
    across = shifted(own, sizes, axis, 2)
    up = shifted(own, sizes, axis, -1)
    down = shifted(own, sizes, axis, 1)
    return jnp.concatenate([own, up]), jnp.concatenate([across, down])


def far_blocks(first, second, sizes, axis):
    first_down = shifted(first, sizes, axis, 1)
    second_up = shifted(second, sizes, axis, -1)
    second_down = shifted(second, sizes, axis, 1)
    first_up = shifted(first, sizes, axis, -1)
    first_across = shifted(first_down, sizes, axis, 1)
    second_across = shifted(second_up, sizes, axis, -1)
    return [
        first, second, first_up, second_up, first_across, second_across, first_down, second_down
    ]


def batched(spec, left, right):
    return jnp.einsum(spec, left, right, precision=EXACT, preferred_element_type=jnp.float32)


def table_kernel(log_row, log_col, residue_row, residue_col, high, low, hops):
    channels, width = high.shape[1:3]
    modes = width // channels
    rate_row, rate_col = jnp.exp(log_row[...]), jnp.exp(log_col[...])
    amp_row = residue_row[...] * jnp.sqrt(2.0 * rate_row)
    amp_col = residue_col[...] * jnp.sqrt(2.0 * rate_col)
    row = lax.broadcasted_iota(jnp.int32, (width, width), 0)
    col = lax.broadcasted_iota(jnp.int32, (width, width), 1)
    row_step, col_step = row.astype(jnp.float32), col.astype(jnp.float32)
    into = jnp.exp(-rate_row * (width - 1.0 - row_step))
    out_of = jnp.exp(-rate_row * (row_step + 1.0))
    into_amp = amp_col * jnp.exp(-rate_col * (width - 1.0 - col_step))
    out_amp = amp_col * jnp.exp(-rate_col * (col_step + 1.0))
    grow = amp_row * jnp.exp(rate_row * row_step)
    fade = jnp.exp(-rate_col * col_step)

    def put(table, c, value):
        rough = value.astype(jnp.bfloat16)
        high[table, c] = rough
        low[table, c] = (value - rough.astype(jnp.float32)).astype(jnp.bfloat16)

    for c in range(channels):
        own_col = (col >= c * modes) & (col < (c + 1) * modes)
        own_row = (row >= c * modes) & (row < (c + 1) * modes)
        near = jnp.dot(
            jnp.where(own_col, grow, 0.0), fade, precision=EXACT, preferred_element_type=jnp.float32
        )
        near = jnp.where(col >= row, near, 0.0)
        put(0, c, jnp.where(own_col, into, 0.0))
        put(1, c, jnp.where(own_col, out_of, 0.0))
        put(2, c, near)
        put(3, c, near.T)
        put(4, c, jnp.where(own_row, out_amp, 0.0))
        put(5, c, jnp.where(own_row, into_amp, 0.0))
    for level in range(hops.shape[0]):
        hops[level : level + 1, :] = jnp.exp(-rate_row * (width * 2.0**level))


def mode_tables(residue_rows, log_rows, width):
    channels, modes = log_rows.shape
    here = pl.BlockSpec(memory_space=pltpu.VMEM)
    tables = jax.ShapeDtypeStruct((6, channels, width, width), jnp.bfloat16)
    return pl.pallas_call(
        table_kernel,
        out_shape=(tables, tables, jax.ShapeDtypeStruct((8, channels * modes), jnp.float32)),
        in_specs=[here] * 4,
        out_specs=(here,) * 3,
        compiler_params=pltpu.CompilerParams(vmem_limit_bytes=24 * 2**20),
    )(
        log_rows.reshape(1, -1),
        log_rows.reshape(-1, 1),
        residue_rows.reshape(1, -1),
        residue_rows.reshape(-1, 1),
    )


def filter_kernel(signal, high, low, hops, filtered, states):
    channels, chunks = signal.shape[1:3]
    modes = hops.shape[1]

    def dot(left, right):
        return jnp.dot(left, right, preferred_element_type=jnp.float32)

    def times(left, table, c):
        return dot(left, high[table, c]) + dot(left, low[table, c])

    head = jnp.zeros((chunks, modes), jnp.float32)
    tail = jnp.zeros((chunks, modes), jnp.float32)
    for c in range(channels):
        head = head + times(signal[0, c], 0, c)
        tail = tail + times(signal[1, c], 1, c)
    place = lax.broadcasted_iota(jnp.int32, (chunks, modes), 0)

    def later(array, step):
        return jnp.where(place >= step, pltpu.roll(array, step, 0), 0.0)

    def earlier(array, step):
        return jnp.where(place < chunks - step, pltpu.roll(array, chunks - step, 0), 0.0)

    ahead, behind = later(head, 1), earlier(tail, 1)
    step, level = 1, 0
    while step < chunks:
        hop = hops[level : level + 1, :]
        ahead = ahead + hop * later(ahead, step)
        behind = behind + hop * earlier(behind, step)
        step, level = 2 * step, level + 1
    states[0], states[1], states[2] = head, tail, ahead
    for which, state in ((0, ahead), (1, behind)):
        rough = state.astype(jnp.bfloat16)
        fine = (state - rough.astype(jnp.float32)).astype(jnp.bfloat16)
        for c in range(channels):
            far = times(rough, 4 + which, c) + dot(fine, high[4 + which, c])
            filtered[which, c] = (times(signal[which, c], 2 + which, c) + far).astype(jnp.bfloat16)


def filter_both(signal, tables):
    chunks, modes = signal.shape[2], tables[2].shape[1]
    return pl.pallas_call(
        filter_kernel,
        out_shape=(
            jax.ShapeDtypeStruct(signal.shape, jnp.bfloat16),
            jax.ShapeDtypeStruct((3, chunks, modes), jnp.float32),
        ),
        in_specs=[pl.BlockSpec(memory_space=pltpu.VMEM)] * 4,
        out_specs=(pl.BlockSpec(memory_space=pltpu.VMEM),) * 2,
        compiler_params=pltpu.CompilerParams(vmem_limit_bytes=24 * 2**20),
        cost_estimate=pl.CostEstimate(flops=200_000_000, bytes_accessed=4_000_000, transcendentals=0),
    )(signal, *tables)


SIDE = 4
COUNT = 4 * SIDE
FLIGHT = (3, 11, 6, 14, 2, 10, 7, 15, 4, 12, 5, 13, 0, 8, 1, 9)


def fetch(blocks, held, arrived):
    copies = [
        pltpu.make_async_copy(blocks[FLIGHT.index(i)], held.at[i], arrived.at[i])
        for i in range(COUNT)
    ]
    for copy in copies:
        copy.start()

    def block(i):
        copies[i].wait()
        return held[i]

    return block


def split_index(i):
    return i // (2 * SIDE), i // 2 % SIDE, i % 2


def project_kernel(place, tokens, cotangent, turn, *refs):
    blocks, (gates, back, sent, held, arrived, total, back_total, turned) = refs[:COUNT], refs[COUNT:]
    width = gates.shape[0]
    block = fetch(blocks, held, arrived)
    deep = turn.shape[0]
    piece = deep // SIDE
    sources = (tokens, cotangent)
    for z1 in range(2):
        for distance in range(SIDE):
            y = lax.rem(place[0] + distance, SIDE)
            start = pl.multiple_of(y * (2 * deep) + z1 * deep, deep)
            for which in range(2):
                turned[which, z1, distance] = jnp.dot(
                    sources[which][:, pl.ds(start, deep)],
                    turn[...],
                    preferred_element_type=jnp.float32,
                ).astype(jnp.bfloat16)

    def columns(which, i):
        z1, far, half = split_index(i)
        if z1 == 0:
            return turned[which, 0, far, :, half * 2 * piece : (half + 1) * 2 * piece]
        lanes = slice(far * piece, (far + 1) * piece)
        return jnp.concatenate(
            [turned[which, 1, 2 * half, :, lanes], turned[which, 1, 2 * half + 1, :, lanes]], axis=1
        )

    for i in range(COUNT):
        rows = block(i)
        term = jnp.dot(columns(0, i), rows[:, : 2 * width], preferred_element_type=jnp.float32)
        back_term = jnp.dot(columns(1, i), rows[:, 2 * width :], preferred_element_type=jnp.float32)
        if i == 0:
            total[...] = term
            back_total[...] = back_term
        else:
            total[...] += term
            back_total[...] += back_term
    gates[...] = total[:, width:].T
    back[...] = back_total[...].T
    sent[0] = total[:, :width].T.astype(jnp.bfloat16)
    sent[1] = (back[...] * gates[...]).astype(jnp.bfloat16)


def held_blocks(blocks):
    return [
        pltpu.VMEM((COUNT,) + blocks[0].shape, blocks[0].dtype),
        pltpu.SemaphoreType.DMA((COUNT,)),
    ]


def project(place, tokens, cotangent, turn, blocks):
    rows = tokens.shape[0]
    width = blocks[0].shape[1] // 3
    here = pl.BlockSpec(memory_space=pltpu.VMEM)
    return pl.pallas_call(
        project_kernel,
        out_shape=(
            jax.ShapeDtypeStruct((width, rows), jnp.float32),
            jax.ShapeDtypeStruct((width, rows), jnp.float32),
            jax.ShapeDtypeStruct((2, width, rows), jnp.bfloat16),
        ),
        in_specs=[pl.BlockSpec(memory_space=pltpu.SMEM), here, here, here]
        + [pl.BlockSpec(memory_space=pl.ANY)] * COUNT,
        out_specs=(here, here, here),
        scratch_shapes=held_blocks(blocks)
        + [
            pltpu.VMEM((rows, 2 * width), jnp.float32),
            pltpu.VMEM((rows, width), jnp.float32),
            pltpu.VMEM((2, 2, SIDE, rows, turn.shape[0]), jnp.bfloat16),
        ],
        compiler_params=pltpu.CompilerParams(vmem_limit_bytes=VMEM_GRANT),
    )(place, tokens, cotangent, turn, *blocks)


def out_kernel(place, gates, back, filtered, *refs):
    blocks, (parts, held, arrived, mixed, grads) = refs[:COUNT], refs[COUNT:]
    width = gates.shape[0]
    block = fetch(blocks, held, arrived)
    conv = filtered[0].astype(jnp.float32)
    mixed[...] = (gates[...] * conv).astype(jnp.bfloat16)
    grads[:width] = filtered[1]
    grads[width:] = (back[...] * conv).astype(jnp.bfloat16)
    deep = held.shape[1]
    for i in range(COUNT):
        z1, far, half = split_index(i)
        rows = block(i)
        outs = (
            jnp.dot(rows[:, 2 * width :], mixed[...], preferred_element_type=jnp.float32),
            jnp.dot(rows[:, : 2 * width], grads[...], preferred_element_type=jnp.float32),
        )
        for which in range(2):
            out = outs[which].T.astype(jnp.bfloat16)
            if z1 == 0:
                y = lax.rem(place[0] + far, SIDE)
                parts[0, y, which, :, half * deep : (half + 1) * deep] = out
            else:
                for part in range(2):
                    y = lax.rem(place[0] + 2 * half + part, SIDE)
                    piece = slice(far * (deep // 2), (far + 1) * (deep // 2))
                    parts[1, y, which, :, piece] = out[:, part * (deep // 2) : (part + 1) * (deep // 2)]


def project_back(place, gates, back, filtered, blocks):
    width, rows = gates.shape
    deep = blocks[0].shape[0]
    here = pl.BlockSpec(memory_space=pltpu.VMEM)
    return pl.pallas_call(
        out_kernel,
        out_shape=jax.ShapeDtypeStruct((2, SIDE, 2, rows, 2 * deep), jnp.bfloat16),
        in_specs=[pl.BlockSpec(memory_space=pltpu.SMEM), here, here, here]
        + [pl.BlockSpec(memory_space=pl.ANY)] * COUNT,
        out_specs=here,
        scratch_shapes=held_blocks(blocks)
        + [
            pltpu.VMEM((width, rows), jnp.bfloat16),
            pltpu.VMEM((2 * width, rows), jnp.bfloat16),
        ],
        compiler_params=pltpu.CompilerParams(vmem_limit_bytes=VMEM_GRANT),
    )(place, gates, back, filtered, *blocks)


def by_chunk(states):
    return states.reshape(-1, states.shape[2]).T


def parameter_grads(signal, grad, head, tail, ahead, residue_rows, log_rows):
    chunks, width = signal.shape[1:]
    rates = jnp.exp(log_rows)
    root = jnp.sqrt(2.0 * rates)
    steps = jnp.arange(width).astype(jnp.float32)
    lag = jnp.maximum(steps[None, :] - steps[:, None], -1.0)[None]
    overlap = jnp.where(lag >= 0.0, batched("cku,ckt->cut", signal, grad), 0.0)
    grow = jnp.exp(rates[:, :, None] * steps[None, None, :])
    fade = jnp.exp(-rates[:, :, None] * steps[None, None, :])
    shape = residue_rows.shape
    plain = jnp.sum(batched("cut,crt->cru", overlap, fade) * grow, axis=2)
    plain = plain + jnp.sum(ahead * tail, axis=0).reshape(shape)
    to_end = (width - 1.0 - steps)[None, None, :]
    from_start = (steps + 1.0)[None, None, :]
    into_moment = jnp.exp(-rates[:, :, None] * to_end) * to_end
    out_moment = jnp.exp(-rates[:, :, None] * from_start) * from_start
    head_moment = by_chunk(batched("cku,cru->crk", signal, into_moment))
    tail_moment = by_chunk(batched("ckt,crt->crk", grad, out_moment))
    blocks = jnp.arange(chunks).astype(jnp.float32)
    gap = (blocks[:, None] - blocks[None, :] - 1.0)[:, :, None]
    hop = width * jnp.maximum(gap, 0.0)
    carry = jnp.where(gap >= 0.0, jnp.exp(-rates.reshape(1, 1, -1) * hop), 0.0)
    ahead_moment = jnp.sum(carry * (head_moment[None] + hop * head[None]), axis=1)
    far = jnp.sum(ahead * tail_moment + ahead_moment * tail, axis=0).reshape(shape)
    moment = jnp.sum(batched("cut,crt->cru", overlap * lag, fade) * grow, axis=2) + far
    return plain * root, residue_rows * root * (0.5 * plain - rates * moment)


def local(tokens, w_value, w_gate, w_output, residues, log_rates, cotangent):
    seq_devices, tp_devices = lax.axis_size("seq"), lax.axis_size("tp")
    sizes, tp_sizes = (SIDE, SIDE, seq_devices // SIDE**2), (tp_devices // 2, 2)
    z_groups = groups_along(sizes, (1,))
    core_groups, line_groups = groups_along(tp_sizes, (1,)), groups_along(tp_sizes, (0,))
    rows, model = tokens.shape
    block, width = w_value.shape
    channels = width // seq_devices
    half = jnp.bfloat16
    me = lax.axis_index("seq")

    weights = jnp.concatenate([w_value, w_gate, w_output.T], axis=1)
    along_z = lax.all_gather(weights, "seq", axis=0, tiled=True, axis_index_groups=z_groups)
    along_z = along_z.reshape(2, 2 * block, 3 * width)
    near = near_blocks(along_z[0], sizes, 2), near_blocks(along_z[1], sizes, 0)
    near = lax.optimization_barrier(near)
    blocks = far_blocks(*near[0], sizes, 0) + far_blocks(*near[1], sizes, 2)

    place = (me // SIDE**2).reshape(1)
    deep = 2 * SIDE * block
    source, target = jnp.arange(deep)[:, None], jnp.arange(deep)[None, :]
    x_wanted = (me + target // (2 * block)) % SIDE
    wanted = target // block % 2 * (SIDE * block) + x_wanted * block + target % block
    turn = (source == wanted).astype(half)
    passed_on = [blocks[i] for i in FLIGHT[:4]]
    passed_on, residues, log_rates = lax.optimization_barrier((passed_on, residues, log_rates))
    residue_rows = residues.reshape(channels, residues.shape[3])
    log_rows = log_rates.reshape(channels, log_rates.shape[3])
    tables = mode_tables(residue_rows, log_rows, rows)
    blocks = [blocks[i] for i in FLIGHT]
    blocks, tables, turn = lax.optimization_barrier((blocks, tables, turn))

    gates, back, sent = project(place, tokens, cotangent, turn, blocks)
    sent = sent.reshape(2, seq_devices, channels, rows).swapaxes(0, 1)
    got = exchange(sent, "seq").transpose(1, 2, 0, 3)
    filtered, states = filter_both(got, tables)
    got_back = exchange(filtered.transpose(2, 0, 1, 3), "seq")
    got_back = got_back.swapaxes(0, 1).reshape(2, width, rows)
    parts = project_back(place, gates, back, got_back, blocks)

    pair = exchange(parts, "tp", core_groups).astype(jnp.float32)
    pair = (pair[0] + pair[1]).astype(half)
    pair, got, states, log_rows = lax.optimization_barrier((pair, got, states, log_rows))
    line = exchange(pair, "tp", line_groups).astype(jnp.float32)
    summed = ((line[0] + line[1]) + (line[2] + line[3])).astype(half)
    result = lax.dot_general(
        summed.reshape(2 * rows, -1), turn, (((1,), (1,)), ((), ())), preferred_element_type=jnp.float32
    )
    result = result.astype(half).reshape(2, rows, model // tp_devices)

    signal, grad = got[0].astype(jnp.float32), got[1].astype(jnp.float32)
    residue_grad, rate_grad = parameter_grads(
        signal, grad, states[0], states[1], states[2], residue_rows, log_rows
    )
    scale = (rows * seq_devices) ** (-0.5)
    return (
        result[0],
        result[1],
        (residue_grad * scale).reshape(residues.shape),
        (rate_grad * scale).reshape(log_rates.shape),
    )


def solution(mesh):
    in_specs = (
        P("seq", None),
        P("seq", "tp"),
        P("seq", "tp"),
        P("tp", "seq"),
        P("tp", "seq", None, None),
        P("tp", "seq", None, None),
        P("seq", None),
    )
    out_specs = (
        P("seq", "tp"),
        P("seq", "tp"),
        P("tp", "seq", None, None),
        P("tp", "seq", None, None),
    )
    return jax.shard_map(local, mesh=mesh, in_specs=in_specs, out_specs=out_specs, check_vma=False)
```

```python
import jax
import jax.numpy as jnp
from jax import lax
from jax.experimental import pallas as pl
from jax.experimental.pallas import tpu as pltpu
from jax.sharding import PartitionSpec as P

EXACT = lax.Precision.HIGHEST
VMEM_GRANT = 56 * 2**20


def groups_along(sizes, picked):
    groups = {}
    total = 1
    for size in sizes:
        total *= size
    for index in range(total):
        rest, coords = index, []
        for size in reversed(sizes):
            coords.append(rest % size)
            rest //= size
        coords.reverse()
        key = tuple(c for axis, c in enumerate(coords) if axis not in picked)
        groups.setdefault(key, []).append(index)
    return list(groups.values())


def exchange(blocks, axis, groups=None):
    return lax.all_to_all(
        blocks, axis, split_axis=0, concat_axis=0, tiled=True, axis_index_groups=groups
    )


def shift_pairs(sizes, axis, step):
    pairs = []
    for group in groups_along(sizes, (axis,)):
        pairs += [(group[i], group[(i + step) % len(group)]) for i in range(len(group))]
    return pairs


def shifted(array, sizes, axis, step):
    return lax.ppermute(array, "seq", shift_pairs(sizes, axis, step))


def near_blocks(own, sizes, axis):
    up = shifted(own, sizes, axis, -1)
    down = shifted(own, sizes, axis, 1)
    across = shifted(up, sizes, axis, -1)
    return jnp.concatenate([own, up]), jnp.concatenate([across, down])


def far_blocks(first, second, sizes, axis):
    first_down = shifted(first, sizes, axis, 1)
    second_up = shifted(second, sizes, axis, -1)
    second_down = shifted(second, sizes, axis, 1)
    first_up = shifted(first, sizes, axis, -1)
    first_across = shifted(first_down, sizes, axis, 1)
    second_across = shifted(second_up, sizes, axis, -1)
    return [
        first, second, first_up, second_up, first_across, second_across, first_down, second_down
    ]


def batched(spec, left, right):
    return jnp.einsum(spec, left, right, precision=EXACT, preferred_element_type=jnp.float32)


def table_kernel(log_row, log_col, residue_row, residue_col, high, low, hops):
    channels, width = high.shape[1:3]
    modes = width // channels
    rate_row, rate_col = jnp.exp(log_row[...]), jnp.exp(log_col[...])
    amp_row = residue_row[...] * jnp.sqrt(2.0 * rate_row)
    amp_col = residue_col[...] * jnp.sqrt(2.0 * rate_col)
    row = lax.broadcasted_iota(jnp.int32, (width, width), 0)
    col = lax.broadcasted_iota(jnp.int32, (width, width), 1)
    row_step, col_step = row.astype(jnp.float32), col.astype(jnp.float32)
    into = jnp.exp(-rate_row * (width - 1.0 - row_step))
    out_of = jnp.exp(-rate_row * (row_step + 1.0))
    into_amp = amp_col * jnp.exp(-rate_col * (width - 1.0 - col_step))
    out_amp = amp_col * jnp.exp(-rate_col * (col_step + 1.0))
    grow = amp_row * jnp.exp(rate_row * row_step)
    fade = jnp.exp(-rate_col * col_step)

    def put(table, c, value):
        rough = value.astype(jnp.bfloat16)
        high[table, c] = rough
        low[table, c] = (value - rough.astype(jnp.float32)).astype(jnp.bfloat16)

    for c in range(channels):
        own_col = (col >= c * modes) & (col < (c + 1) * modes)
        own_row = (row >= c * modes) & (row < (c + 1) * modes)
        near = jnp.dot(
            jnp.where(own_col, grow, 0.0), fade, precision=EXACT, preferred_element_type=jnp.float32
        )
        near = jnp.where(col >= row, near, 0.0)
        put(0, c, jnp.where(own_col, into, 0.0))
        put(1, c, jnp.where(own_col, out_of, 0.0))
        put(2, c, near)
        put(3, c, near.T)
        put(4, c, jnp.where(own_row, out_amp, 0.0))
        put(5, c, jnp.where(own_row, into_amp, 0.0))
    for level in range(hops.shape[0]):
        hops[level : level + 1, :] = jnp.exp(-rate_row * (width * 2.0**level))


def mode_tables(residue_rows, log_rows, width):
    channels, modes = log_rows.shape
    here = pl.BlockSpec(memory_space=pltpu.VMEM)
    tables = jax.ShapeDtypeStruct((6, channels, width, width), jnp.bfloat16)
    return pl.pallas_call(
        table_kernel,
        out_shape=(tables, tables, jax.ShapeDtypeStruct((8, channels * modes), jnp.float32)),
        in_specs=[here] * 4,
        out_specs=(here,) * 3,
        compiler_params=pltpu.CompilerParams(vmem_limit_bytes=24 * 2**20),
    )(
        log_rows.reshape(1, -1),
        log_rows.reshape(-1, 1),
        residue_rows.reshape(1, -1),
        residue_rows.reshape(-1, 1),
    )


def filter_kernel(signal, high, low, hops, filtered, states):
    channels, chunks = signal.shape[1:3]
    modes = hops.shape[1]

    def dot(left, right):
        return jnp.dot(left, right, preferred_element_type=jnp.float32)

    def times(left, table, c):
        return dot(left, high[table, c]) + dot(left, low[table, c])

    head = jnp.zeros((chunks, modes), jnp.float32)
    tail = jnp.zeros((chunks, modes), jnp.float32)
    for c in range(channels):
        head = head + times(signal[0, c], 0, c)
        tail = tail + times(signal[1, c], 1, c)
    place = lax.broadcasted_iota(jnp.int32, (chunks, modes), 0)

    def later(array, step):
        return jnp.where(place >= step, pltpu.roll(array, step, 0), 0.0)

    def earlier(array, step):
        return jnp.where(place < chunks - step, pltpu.roll(array, chunks - step, 0), 0.0)

    ahead, behind = later(head, 1), earlier(tail, 1)
    step, level = 1, 0
    while step < chunks:
        hop = hops[level : level + 1, :]
        ahead = ahead + hop * later(ahead, step)
        behind = behind + hop * earlier(behind, step)
        step, level = 2 * step, level + 1
    states[0], states[1], states[2] = head, tail, ahead
    for which, state in ((0, ahead), (1, behind)):
        rough = state.astype(jnp.bfloat16)
        fine = (state - rough.astype(jnp.float32)).astype(jnp.bfloat16)
        for c in range(channels):
            far = times(rough, 4 + which, c) + dot(fine, high[4 + which, c])
            filtered[which, c] = (times(signal[which, c], 2 + which, c) + far).astype(jnp.bfloat16)


def filter_both(signal, tables):
    chunks, modes = signal.shape[2], tables[2].shape[1]
    return pl.pallas_call(
        filter_kernel,
        out_shape=(
            jax.ShapeDtypeStruct(signal.shape, jnp.bfloat16),
            jax.ShapeDtypeStruct((3, chunks, modes), jnp.float32),
        ),
        in_specs=[pl.BlockSpec(memory_space=pltpu.VMEM)] * 4,
        out_specs=(pl.BlockSpec(memory_space=pltpu.VMEM),) * 2,
        compiler_params=pltpu.CompilerParams(vmem_limit_bytes=24 * 2**20),
        cost_estimate=pl.CostEstimate(flops=200_000_000, bytes_accessed=4_000_000, transcendentals=0),
    )(signal, *tables)


SIDE = 4
COUNT = 4 * SIDE
FLIGHT = (3, 11, 6, 14, 2, 10, 7, 15, 4, 12, 5, 13, 0, 8, 1, 9)


def fetch(blocks, held, arrived):
    copies = [
        pltpu.make_async_copy(blocks[FLIGHT.index(i)], held.at[i], arrived.at[i])
        for i in range(COUNT)
    ]
    for copy in copies:
        copy.start()

    def block(i):
        copies[i].wait()
        return held[i]

    return block


def split_index(i):
    return i // (2 * SIDE), i // 2 % SIDE, i % 2


def project_kernel(place, tokens, cotangent, turn, *refs):
    blocks, (gates, back, sent, held, arrived, total, back_total, turned) = refs[:COUNT], refs[COUNT:]
    width = gates.shape[0]
    block = fetch(blocks, held, arrived)
    deep = turn.shape[0]
    piece = deep // SIDE
    sources = (tokens, cotangent)
    for z1 in range(2):
        for distance in range(SIDE):
            y = lax.rem(place[0] + distance, SIDE)
            start = pl.multiple_of(y * (2 * deep) + z1 * deep, deep)
            for which in range(2):
                turned[which, z1, distance] = jnp.dot(
                    sources[which][:, pl.ds(start, deep)],
                    turn[...],
                    preferred_element_type=jnp.float32,
                ).astype(jnp.bfloat16)

    def columns(which, i):
        z1, far, half = split_index(i)
        if z1 == 0:
            return turned[which, 0, far, :, half * 2 * piece : (half + 1) * 2 * piece]
        lanes = slice(far * piece, (far + 1) * piece)
        return jnp.concatenate(
            [turned[which, 1, 2 * half, :, lanes], turned[which, 1, 2 * half + 1, :, lanes]], axis=1
        )

    for i in range(COUNT):
        rows = block(i)
        term = jnp.dot(columns(0, i), rows[:, : 2 * width], preferred_element_type=jnp.float32)
        back_term = jnp.dot(columns(1, i), rows[:, 2 * width :], preferred_element_type=jnp.float32)
        if i == 0:
            total[...] = term
            back_total[...] = back_term
        else:
            total[...] += term
            back_total[...] += back_term
    gates[...] = total[:, width:].T
    back[...] = back_total[...].T
    sent[0] = total[:, :width].T.astype(jnp.bfloat16)
    sent[1] = (back[...] * gates[...]).astype(jnp.bfloat16)


def held_blocks(blocks):
    return [
        pltpu.VMEM((COUNT,) + blocks[0].shape, blocks[0].dtype),
        pltpu.SemaphoreType.DMA((COUNT,)),
    ]


def project(place, tokens, cotangent, turn, blocks):
    rows = tokens.shape[0]
    width = blocks[0].shape[1] // 3
    here = pl.BlockSpec(memory_space=pltpu.VMEM)
    return pl.pallas_call(
        project_kernel,
        out_shape=(
            jax.ShapeDtypeStruct((width, rows), jnp.float32),
            jax.ShapeDtypeStruct((width, rows), jnp.float32),
            jax.ShapeDtypeStruct((2, width, rows), jnp.bfloat16),
        ),
        in_specs=[pl.BlockSpec(memory_space=pltpu.SMEM), here, here, here]
        + [pl.BlockSpec(memory_space=pl.ANY)] * COUNT,
        out_specs=(here, here, here),
        scratch_shapes=held_blocks(blocks)
        + [
            pltpu.VMEM((rows, 2 * width), jnp.float32),
            pltpu.VMEM((rows, width), jnp.float32),
            pltpu.VMEM((2, 2, SIDE, rows, turn.shape[0]), jnp.bfloat16),
        ],
        compiler_params=pltpu.CompilerParams(vmem_limit_bytes=VMEM_GRANT),
    )(place, tokens, cotangent, turn, *blocks)


def out_kernel(place, gates, back, filtered, *refs):
    blocks, (parts, held, arrived, mixed, grads) = refs[:COUNT], refs[COUNT:]
    width = gates.shape[0]
    block = fetch(blocks, held, arrived)
    conv = filtered[0].astype(jnp.float32)
    mixed[...] = (gates[...] * conv).astype(jnp.bfloat16)
    grads[:width] = filtered[1]
    grads[width:] = (back[...] * conv).astype(jnp.bfloat16)
    deep = held.shape[1]
    for i in range(COUNT):
        z1, far, half = split_index(i)
        rows = block(i)
        outs = (
            jnp.dot(rows[:, 2 * width :], mixed[...], preferred_element_type=jnp.float32),
            jnp.dot(rows[:, : 2 * width], grads[...], preferred_element_type=jnp.float32),
        )
        for which in range(2):
            out = outs[which].T.astype(jnp.bfloat16)
            if z1 == 0:
                y = lax.rem(place[0] + far, SIDE)
                parts[0, y, which, :, half * deep : (half + 1) * deep] = out
            else:
                for part in range(2):
                    y = lax.rem(place[0] + 2 * half + part, SIDE)
                    piece = slice(far * (deep // 2), (far + 1) * (deep // 2))
                    parts[1, y, which, :, piece] = out[:, part * (deep // 2) : (part + 1) * (deep // 2)]


def project_back(place, gates, back, filtered, blocks):
    width, rows = gates.shape
    deep = blocks[0].shape[0]
    here = pl.BlockSpec(memory_space=pltpu.VMEM)
    return pl.pallas_call(
        out_kernel,
        out_shape=jax.ShapeDtypeStruct((2, SIDE, 2, rows, 2 * deep), jnp.bfloat16),
        in_specs=[pl.BlockSpec(memory_space=pltpu.SMEM), here, here, here]
        + [pl.BlockSpec(memory_space=pl.ANY)] * COUNT,
        out_specs=here,
        scratch_shapes=held_blocks(blocks)
        + [
            pltpu.VMEM((width, rows), jnp.bfloat16),
            pltpu.VMEM((2 * width, rows), jnp.bfloat16),
        ],
        compiler_params=pltpu.CompilerParams(vmem_limit_bytes=VMEM_GRANT),
    )(place, gates, back, filtered, *blocks)


def by_chunk(states):
    return states.reshape(-1, states.shape[2]).T


def parameter_grads(signal, grad, head, tail, ahead, residue_rows, log_rows):
    chunks, width = signal.shape[1:]
    rates = jnp.exp(log_rows)
    root = jnp.sqrt(2.0 * rates)
    steps = jnp.arange(width).astype(jnp.float32)
    lag = jnp.maximum(steps[None, :] - steps[:, None], -1.0)[None]
    overlap = jnp.where(lag >= 0.0, batched("cku,ckt->cut", signal, grad), 0.0)
    grow = jnp.exp(rates[:, :, None] * steps[None, None, :])
    fade = jnp.exp(-rates[:, :, None] * steps[None, None, :])
    shape = residue_rows.shape
    plain = jnp.sum(batched("cut,crt->cru", overlap, fade) * grow, axis=2)
    plain = plain + jnp.sum(ahead * tail, axis=0).reshape(shape)
    to_end = (width - 1.0 - steps)[None, None, :]
    from_start = (steps + 1.0)[None, None, :]
    into_moment = jnp.exp(-rates[:, :, None] * to_end) * to_end
    out_moment = jnp.exp(-rates[:, :, None] * from_start) * from_start
    head_moment = by_chunk(batched("cku,cru->crk", signal, into_moment))
    tail_moment = by_chunk(batched("ckt,crt->crk", grad, out_moment))
    blocks = jnp.arange(chunks).astype(jnp.float32)
    gap = (blocks[:, None] - blocks[None, :] - 1.0)[:, :, None]
    hop = width * jnp.maximum(gap, 0.0)
    carry = jnp.where(gap >= 0.0, jnp.exp(-rates.reshape(1, 1, -1) * hop), 0.0)
    ahead_moment = jnp.sum(carry * (head_moment[None] + hop * head[None]), axis=1)
    far = jnp.sum(ahead * tail_moment + ahead_moment * tail, axis=0).reshape(shape)
    moment = jnp.sum(batched("cut,crt->cru", overlap * lag, fade) * grow, axis=2) + far
    return plain * root, residue_rows * root * (0.5 * plain - rates * moment)


def local(tokens, w_value, w_gate, w_output, residues, log_rates, cotangent):
    seq_devices, tp_devices = lax.axis_size("seq"), lax.axis_size("tp")
    sizes, tp_sizes = (SIDE, SIDE, seq_devices // SIDE**2), (tp_devices // 2, 2)
    z_groups = groups_along(sizes, (1,))
    core_groups, line_groups = groups_along(tp_sizes, (1,)), groups_along(tp_sizes, (0,))
    rows, model = tokens.shape
    block, width = w_value.shape
    channels = width // seq_devices
    half = jnp.bfloat16
    me = lax.axis_index("seq")

    weights = jnp.concatenate([w_value, w_gate, w_output.T], axis=1)
    along_z = lax.all_gather(weights, "seq", axis=0, tiled=True, axis_index_groups=z_groups)
    along_z = along_z.reshape(2, 2 * block, 3 * width)
    near = near_blocks(along_z[0], sizes, 2), near_blocks(along_z[1], sizes, 0)
    near = lax.optimization_barrier(near)
    blocks = far_blocks(*near[0], sizes, 0) + far_blocks(*near[1], sizes, 2)

    place = (me // SIDE**2).reshape(1)
    deep = 2 * SIDE * block
    source, target = jnp.arange(deep)[:, None], jnp.arange(deep)[None, :]
    x_wanted = (me + target // (2 * block)) % SIDE
    wanted = target // block % 2 * (SIDE * block) + x_wanted * block + target % block
    turn = (source == wanted).astype(half)
    passed_on = [blocks[i] for i in FLIGHT[:4]]
    passed_on, residues, log_rates = lax.optimization_barrier((passed_on, residues, log_rates))
    residue_rows = residues.reshape(channels, residues.shape[3])
    log_rows = log_rates.reshape(channels, log_rates.shape[3])
    tables = mode_tables(residue_rows, log_rows, rows)
    blocks = [blocks[i] for i in FLIGHT]
    blocks, tables, turn = lax.optimization_barrier((blocks, tables, turn))

    gates, back, sent = project(place, tokens, cotangent, turn, blocks)
    sent = sent.reshape(2, seq_devices, channels, rows).swapaxes(0, 1)
    got = exchange(sent, "seq").transpose(1, 2, 0, 3)
    filtered, states = filter_both(got, tables)
    got_back = exchange(filtered.transpose(2, 0, 1, 3), "seq")
    got_back = got_back.swapaxes(0, 1).reshape(2, width, rows)
    parts = project_back(place, gates, back, got_back, blocks)

    pair = exchange(parts, "tp", core_groups).astype(jnp.float32)
    pair = (pair[0] + pair[1]).astype(half)
    pair, got, states, log_rows = lax.optimization_barrier((pair, got, states, log_rows))
    line = exchange(pair, "tp", line_groups).astype(jnp.float32)
    summed = ((line[0] + line[1]) + (line[2] + line[3])).astype(half)
    result = lax.dot_general(
        summed.reshape(2 * rows, -1), turn, (((1,), (1,)), ((), ())), preferred_element_type=jnp.float32
    )
    result = result.astype(half).reshape(2, rows, model // tp_devices)

    signal, grad = got[0].astype(jnp.float32), got[1].astype(jnp.float32)
    residue_grad, rate_grad = parameter_grads(
        signal, grad, states[0], states[1], states[2], residue_rows, log_rows
    )
    scale = (rows * seq_devices) ** (-0.5)
    return (
        result[0],
        result[1],
        (residue_grad * scale).reshape(residues.shape),
        (rate_grad * scale).reshape(log_rates.shape),
    )


def solution(mesh):
    in_specs = (
        P("seq", None),
        P("seq", "tp"),
        P("seq", "tp"),
        P("tp", "seq"),
        P("tp", "seq", None, None),
        P("tp", "seq", None, None),
        P("seq", None),
    )
    out_specs = (
        P("seq", "tp"),
        P("seq", "tp"),
        P("tp", "seq", None, None),
        P("tp", "seq", None, None),
    )
    return jax.shard_map(local, mesh=mesh, in_specs=in_specs, out_specs=out_specs, check_vma=False)
```

```python
import jax
import jax.numpy as jnp
from jax import lax
from jax.experimental import pallas as pl
from jax.experimental.pallas import tpu as pltpu
from jax.sharding import PartitionSpec as P

EXACT = lax.Precision.HIGHEST
VMEM_GRANT = 56 * 2**20


def groups_along(sizes, picked):
    groups = {}
    total = 1
    for size in sizes:
        total *= size
    for index in range(total):
        rest, coords = index, []
        for size in reversed(sizes):
            coords.append(rest % size)
            rest //= size
        coords.reverse()
        key = tuple(c for axis, c in enumerate(coords) if axis not in picked)
        groups.setdefault(key, []).append(index)
    return list(groups.values())


def exchange(blocks, axis, groups=None):
    return lax.all_to_all(
        blocks, axis, split_axis=0, concat_axis=0, tiled=True, axis_index_groups=groups
    )


def shift_pairs(sizes, axis, step):
    pairs = []
    for group in groups_along(sizes, (axis,)):
        pairs += [(group[i], group[(i + step) % len(group)]) for i in range(len(group))]
    return pairs


def shifted(array, sizes, axis, step):
    return lax.ppermute(array, "seq", shift_pairs(sizes, axis, step))


def near_blocks(own, sizes, axis):
    up = shifted(own, sizes, axis, -1)
    down = shifted(own, sizes, axis, 1)
    across = shifted(up, sizes, axis, -1)
    return jnp.concatenate([own, up]), jnp.concatenate([across, down])


def far_blocks(first, second, sizes, axis):
    first_down = shifted(first, sizes, axis, 1)
    second_up = shifted(second, sizes, axis, -1)
    second_down = shifted(second, sizes, axis, 1)
    first_up = shifted(first, sizes, axis, -1)
    first_across = shifted(first_down, sizes, axis, 1)
    second_across = shifted(second_up, sizes, axis, -1)
    return [
        first, second, first_up, second_up, first_across, second_across, first_down, second_down
    ]


def batched(spec, left, right):
    return jnp.einsum(spec, left, right, precision=EXACT, preferred_element_type=jnp.float32)


def table_kernel(log_row, log_col, residue_row, residue_col, high, low, hops):
    channels, width = high.shape[1:3]
    modes = width // channels
    rate_row, rate_col = jnp.exp(log_row[...]), jnp.exp(log_col[...])
    amp_row = residue_row[...] * jnp.sqrt(2.0 * rate_row)
    amp_col = residue_col[...] * jnp.sqrt(2.0 * rate_col)
    row = lax.broadcasted_iota(jnp.int32, (width, width), 0)
    col = lax.broadcasted_iota(jnp.int32, (width, width), 1)
    row_step, col_step = row.astype(jnp.float32), col.astype(jnp.float32)
    into = jnp.exp(-rate_row * (width - 1.0 - row_step))
    out_of = jnp.exp(-rate_row * (row_step + 1.0))
    into_amp = amp_col * jnp.exp(-rate_col * (width - 1.0 - col_step))
    out_amp = amp_col * jnp.exp(-rate_col * (col_step + 1.0))
    grow = amp_row * jnp.exp(rate_row * row_step)
    fade = jnp.exp(-rate_col * col_step)

    def put(table, c, value):
        rough = value.astype(jnp.bfloat16)
        high[table, c] = rough
        low[table, c] = (value - rough.astype(jnp.float32)).astype(jnp.bfloat16)

    for c in range(channels):
        own_col = (col >= c * modes) & (col < (c + 1) * modes)
        own_row = (row >= c * modes) & (row < (c + 1) * modes)
        near = jnp.dot(
            jnp.where(own_col, grow, 0.0), fade, precision=EXACT, preferred_element_type=jnp.float32
        )
        near = jnp.where(col >= row, near, 0.0)
        put(0, c, jnp.where(own_col, into, 0.0))
        put(1, c, jnp.where(own_col, out_of, 0.0))
        put(2, c, near)
        put(3, c, near.T)
        put(4, c, jnp.where(own_row, out_amp, 0.0))
        put(5, c, jnp.where(own_row, into_amp, 0.0))
    for level in range(hops.shape[0]):
        hops[level : level + 1, :] = jnp.exp(-rate_row * (width * 2.0**level))


def mode_tables(residue_rows, log_rows, width):
    channels, modes = log_rows.shape
    here = pl.BlockSpec(memory_space=pltpu.VMEM)
    tables = jax.ShapeDtypeStruct((6, channels, width, width), jnp.bfloat16)
    return pl.pallas_call(
        table_kernel,
        out_shape=(tables, tables, jax.ShapeDtypeStruct((8, channels * modes), jnp.float32)),
        in_specs=[here] * 4,
        out_specs=(here,) * 3,
        compiler_params=pltpu.CompilerParams(vmem_limit_bytes=24 * 2**20),
    )(
        log_rows.reshape(1, -1),
        log_rows.reshape(-1, 1),
        residue_rows.reshape(1, -1),
        residue_rows.reshape(-1, 1),
    )


def filter_kernel(signal, high, low, hops, filtered, states):
    channels, chunks = signal.shape[1:3]
    modes = hops.shape[1]

    def dot(left, right):
        return jnp.dot(left, right, preferred_element_type=jnp.float32)

    def times(left, table, c):
        return dot(left, high[table, c]) + dot(left, low[table, c])

    head = jnp.zeros((chunks, modes), jnp.float32)
    tail = jnp.zeros((chunks, modes), jnp.float32)
    for c in range(channels):
        head = head + times(signal[0, c], 0, c)
        tail = tail + times(signal[1, c], 1, c)
    place = lax.broadcasted_iota(jnp.int32, (chunks, modes), 0)

    def later(array, step):
        return jnp.where(place >= step, pltpu.roll(array, step, 0), 0.0)

    def earlier(array, step):
        return jnp.where(place < chunks - step, pltpu.roll(array, chunks - step, 0), 0.0)

    ahead, behind = later(head, 1), earlier(tail, 1)
    step, level = 1, 0
    while step < chunks:
        hop = hops[level : level + 1, :]
        ahead = ahead + hop * later(ahead, step)
        behind = behind + hop * earlier(behind, step)
        step, level = 2 * step, level + 1
    states[0], states[1], states[2] = head, tail, ahead
    for which, state in ((0, ahead), (1, behind)):
        rough = state.astype(jnp.bfloat16)
        fine = (state - rough.astype(jnp.float32)).astype(jnp.bfloat16)
        for c in range(channels):
            far = times(rough, 4 + which, c) + dot(fine, high[4 + which, c])
            filtered[which, c] = (times(signal[which, c], 2 + which, c) + far).astype(jnp.bfloat16)


def filter_both(signal, tables):
    chunks, modes = signal.shape[2], tables[2].shape[1]
    return pl.pallas_call(
        filter_kernel,
        out_shape=(
            jax.ShapeDtypeStruct(signal.shape, jnp.bfloat16),
            jax.ShapeDtypeStruct((3, chunks, modes), jnp.float32),
        ),
        in_specs=[pl.BlockSpec(memory_space=pltpu.VMEM)] * 4,
        out_specs=(pl.BlockSpec(memory_space=pltpu.VMEM),) * 2,
        compiler_params=pltpu.CompilerParams(vmem_limit_bytes=24 * 2**20),
        cost_estimate=pl.CostEstimate(flops=200_000_000, bytes_accessed=4_000_000, transcendentals=0),
    )(signal, *tables)


SIDE = 4
COUNT = 4 * SIDE
FLIGHT = (3, 11, 6, 14, 2, 10, 7, 15, 4, 12, 5, 13, 0, 8, 1, 9)


def fetch(blocks, held, arrived):
    copies = [
        pltpu.make_async_copy(blocks[FLIGHT.index(i)], held.at[i], arrived.at[i])
        for i in range(COUNT)
    ]
    for copy in copies:
        copy.start()

    def block(i):
        copies[i].wait()
        return held[i]

    return block


def split_index(i):
    return i // (2 * SIDE), i // 2 % SIDE, i % 2


def project_kernel(place, tokens, cotangent, turn, *refs):
    blocks, (gates, back, sent, held, arrived, total, back_total, turned) = refs[:COUNT], refs[COUNT:]
    width = gates.shape[0]
    block = fetch(blocks, held, arrived)
    deep = turn.shape[0]
    piece = deep // SIDE
    sources = (tokens, cotangent)
    for z1 in range(2):
        for distance in range(SIDE):
            y = lax.rem(place[0] + distance, SIDE)
            start = pl.multiple_of(y * (2 * deep) + z1 * deep, deep)
            for which in range(2):
                turned[which, z1, distance] = jnp.dot(
                    sources[which][:, pl.ds(start, deep)],
                    turn[...],
                    preferred_element_type=jnp.float32,
                ).astype(jnp.bfloat16)

    def columns(which, i):
        z1, far, half = split_index(i)
        if z1 == 0:
            return turned[which, 0, far, :, half * 2 * piece : (half + 1) * 2 * piece]
        lanes = slice(far * piece, (far + 1) * piece)
        return jnp.concatenate(
            [turned[which, 1, 2 * half, :, lanes], turned[which, 1, 2 * half + 1, :, lanes]], axis=1
        )

    for i in range(COUNT):
        rows = block(i)
        term = jnp.dot(columns(0, i), rows[:, : 2 * width], preferred_element_type=jnp.float32)
        back_term = jnp.dot(columns(1, i), rows[:, 2 * width :], preferred_element_type=jnp.float32)
        if i == 0:
            total[...] = term
            back_total[...] = back_term
        else:
            total[...] += term
            back_total[...] += back_term
    gates[...] = total[:, width:].T
    back[...] = back_total[...].T
    sent[0] = total[:, :width].T.astype(jnp.bfloat16)
    sent[1] = (back[...] * gates[...]).astype(jnp.bfloat16)


def held_blocks(blocks):
    return [
        pltpu.VMEM((COUNT,) + blocks[0].shape, blocks[0].dtype),
        pltpu.SemaphoreType.DMA((COUNT,)),
    ]


def project(place, tokens, cotangent, turn, blocks):
    rows = tokens.shape[0]
    width = blocks[0].shape[1] // 3
    here = pl.BlockSpec(memory_space=pltpu.VMEM)
    return pl.pallas_call(
        project_kernel,
        out_shape=(
            jax.ShapeDtypeStruct((width, rows), jnp.float32),
            jax.ShapeDtypeStruct((width, rows), jnp.float32),
            jax.ShapeDtypeStruct((2, width, rows), jnp.bfloat16),
        ),
        in_specs=[pl.BlockSpec(memory_space=pltpu.SMEM), here, here, here]
        + [pl.BlockSpec(memory_space=pl.ANY)] * COUNT,
        out_specs=(here, here, here),
        scratch_shapes=held_blocks(blocks)
        + [
            pltpu.VMEM((rows, 2 * width), jnp.float32),
            pltpu.VMEM((rows, width), jnp.float32),
            pltpu.VMEM((2, 2, SIDE, rows, turn.shape[0]), jnp.bfloat16),
        ],
        compiler_params=pltpu.CompilerParams(vmem_limit_bytes=VMEM_GRANT),
    )(place, tokens, cotangent, turn, *blocks)


def out_kernel(place, gates, back, filtered, *refs):
    blocks, (parts, held, arrived, mixed, grads) = refs[:COUNT], refs[COUNT:]
    width = gates.shape[0]
    block = fetch(blocks, held, arrived)
    conv = filtered[0].astype(jnp.float32)
    mixed[...] = (gates[...] * conv).astype(jnp.bfloat16)
    grads[:width] = filtered[1]
    grads[width:] = (back[...] * conv).astype(jnp.bfloat16)
    deep = held.shape[1]
    for i in range(COUNT):
        z1, far, half = split_index(i)
        rows = block(i)
        outs = (
            jnp.dot(rows[:, 2 * width :], mixed[...], preferred_element_type=jnp.float32),
            jnp.dot(rows[:, : 2 * width], grads[...], preferred_element_type=jnp.float32),
        )
        for which in range(2):
            out = outs[which].T.astype(jnp.bfloat16)
            if z1 == 0:
                y = lax.rem(place[0] + far, SIDE)
                parts[0, y, which, :, half * deep : (half + 1) * deep] = out
            else:
                for part in range(2):
                    y = lax.rem(place[0] + 2 * half + part, SIDE)
                    piece = slice(far * (deep // 2), (far + 1) * (deep // 2))
                    parts[1, y, which, :, piece] = out[:, part * (deep // 2) : (part + 1) * (deep // 2)]


def project_back(place, gates, back, filtered, blocks):
    width, rows = gates.shape
    deep = blocks[0].shape[0]
    here = pl.BlockSpec(memory_space=pltpu.VMEM)
    return pl.pallas_call(
        out_kernel,
        out_shape=jax.ShapeDtypeStruct((2, SIDE, 2, rows, 2 * deep), jnp.bfloat16),
        in_specs=[pl.BlockSpec(memory_space=pltpu.SMEM), here, here, here]
        + [pl.BlockSpec(memory_space=pl.ANY)] * COUNT,
        out_specs=here,
        scratch_shapes=held_blocks(blocks)
        + [
            pltpu.VMEM((width, rows), jnp.bfloat16),
            pltpu.VMEM((2 * width, rows), jnp.bfloat16),
        ],
        compiler_params=pltpu.CompilerParams(vmem_limit_bytes=VMEM_GRANT),
    )(place, gates, back, filtered, *blocks)


def by_chunk(states):
    return states.reshape(-1, states.shape[2]).T


def parameter_grads(signal, grad, head, tail, ahead, residue_rows, log_rows):
    chunks, width = signal.shape[1:]
    rates = jnp.exp(log_rows)
    root = jnp.sqrt(2.0 * rates)
    steps = jnp.arange(width).astype(jnp.float32)
    lag = jnp.maximum(steps[None, :] - steps[:, None], -1.0)[None]
    overlap = jnp.where(lag >= 0.0, batched("cku,ckt->cut", signal, grad), 0.0)
    grow = jnp.exp(rates[:, :, None] * steps[None, None, :])
    fade = jnp.exp(-rates[:, :, None] * steps[None, None, :])
    shape = residue_rows.shape
    plain = jnp.sum(batched("cut,crt->cru", overlap, fade) * grow, axis=2)
    plain = plain + jnp.sum(ahead * tail, axis=0).reshape(shape)
    to_end = (width - 1.0 - steps)[None, None, :]
    from_start = (steps + 1.0)[None, None, :]
    into_moment = jnp.exp(-rates[:, :, None] * to_end) * to_end
    out_moment = jnp.exp(-rates[:, :, None] * from_start) * from_start
    head_moment = by_chunk(batched("cku,cru->crk", signal, into_moment))
    tail_moment = by_chunk(batched("ckt,crt->crk", grad, out_moment))
    blocks = jnp.arange(chunks).astype(jnp.float32)
    gap = (blocks[:, None] - blocks[None, :] - 1.0)[:, :, None]
    hop = width * jnp.maximum(gap, 0.0)
    carry = jnp.where(gap >= 0.0, jnp.exp(-rates.reshape(1, 1, -1) * hop), 0.0)
    ahead_moment = jnp.sum(carry * (head_moment[None] + hop * head[None]), axis=1)
    far = jnp.sum(ahead * tail_moment + ahead_moment * tail, axis=0).reshape(shape)
    moment = jnp.sum(batched("cut,crt->cru", overlap * lag, fade) * grow, axis=2) + far
    return plain * root, residue_rows * root * (0.5 * plain - rates * moment)


def local(tokens, w_value, w_gate, w_output, residues, log_rates, cotangent):
    seq_devices, tp_devices = lax.axis_size("seq"), lax.axis_size("tp")
    sizes, tp_sizes = (SIDE, SIDE, seq_devices // SIDE**2), (tp_devices // 2, 2)
    z_groups = groups_along(sizes, (1,))
    core_groups, line_groups = groups_along(tp_sizes, (1,)), groups_along(tp_sizes, (0,))
    rows, model = tokens.shape
    block, width = w_value.shape
    channels = width // seq_devices
    half = jnp.bfloat16
    me = lax.axis_index("seq")

    weights = jnp.concatenate([w_value, w_gate, w_output.T], axis=1)
    along_z = lax.all_gather(weights, "seq", axis=0, tiled=True, axis_index_groups=z_groups)
    along_z = along_z.reshape(2, 2 * block, 3 * width)
    near = near_blocks(along_z[0], sizes, 2), near_blocks(along_z[1], sizes, 0)
    near = [lax.optimization_barrier(pair) for pair in near]
    blocks = far_blocks(*near[0], sizes, 0) + far_blocks(*near[1], sizes, 2)

    place = (me // SIDE**2).reshape(1)
    deep = 2 * SIDE * block
    source, target = jnp.arange(deep)[:, None], jnp.arange(deep)[None, :]
    x_wanted = (me + target // (2 * block)) % SIDE
    wanted = target // block % 2 * (SIDE * block) + x_wanted * block + target % block
    turn = (source == wanted).astype(half)
    passed_on = [blocks[i] for i in FLIGHT[:4]]
    passed_on, residues, log_rates = lax.optimization_barrier((passed_on, residues, log_rates))
    residue_rows = residues.reshape(channels, residues.shape[3])
    log_rows = log_rates.reshape(channels, log_rates.shape[3])
    tables = mode_tables(residue_rows, log_rows, rows)
    blocks = [blocks[i] for i in FLIGHT]
    blocks, tables, turn = lax.optimization_barrier((blocks, tables, turn))

    gates, back, sent = project(place, tokens, cotangent, turn, blocks)
    sent = sent.reshape(2, seq_devices, channels, rows).swapaxes(0, 1)
    got = exchange(sent, "seq").transpose(1, 2, 0, 3)
    filtered, states = filter_both(got, tables)
    got_back = exchange(filtered.transpose(2, 0, 1, 3), "seq")
    got_back = got_back.swapaxes(0, 1).reshape(2, width, rows)
    parts = project_back(place, gates, back, got_back, blocks)

    pair = exchange(parts, "tp", core_groups).astype(jnp.float32)
    pair = (pair[0] + pair[1]).astype(half)
    pair, got, states, log_rows = lax.optimization_barrier((pair, got, states, log_rows))
    line = exchange(pair, "tp", line_groups).astype(jnp.float32)
    summed = ((line[0] + line[1]) + (line[2] + line[3])).astype(half)
    result = lax.dot_general(
        summed.reshape(2 * rows, -1), turn, (((1,), (1,)), ((), ())), preferred_element_type=jnp.float32
    )
    result = result.astype(half).reshape(2, rows, model // tp_devices)

    signal, grad = got[0].astype(jnp.float32), got[1].astype(jnp.float32)
    residue_grad, rate_grad = parameter_grads(
        signal, grad, states[0], states[1], states[2], residue_rows, log_rows
    )
    scale = (rows * seq_devices) ** (-0.5)
    return (
        result[0],
        result[1],
        (residue_grad * scale).reshape(residues.shape),
        (rate_grad * scale).reshape(log_rates.shape),
    )


def solution(mesh):
    in_specs = (
        P("seq", None),
        P("seq", "tp"),
        P("seq", "tp"),
        P("tp", "seq"),
        P("tp", "seq", None, None),
        P("tp", "seq", None, None),
        P("seq", None),
    )
    out_specs = (
        P("seq", "tp"),
        P("seq", "tp"),
        P("tp", "seq", None, None),
        P("tp", "seq", None, None),
    )
    return jax.shard_map(local, mesh=mesh, in_specs=in_specs, out_specs=out_specs, check_vma=False)
```
